32 devices in a mesh: dp: 4 (over x, core), fsdp: 8 (over z, y).
Axes of the slice: x: 2, y: 2, z: 4, core: 2. Of those that a mesh axis runs over, the one named last changes fastest.
Arguments:
- latent: bfloat16 [8192, 512], P(('dp', 'fsdp')), may hold values from -6 to 6
- cotangent: bfloat16 [8192, 16384], P(('dp', 'fsdp')), may hold values from -2 to 2
- quant: bfloat16 [512, 16384], P(None, 'fsdp'), may hold values from -6 to 6
- scales: float32 [4, 128], P(None, 'fsdp'), may hold values from 0.015 to 0.09
- adapter_down: bfloat16 [512, 64], replicated, may hold values from -0.25 to 0.25
- adapter_up: bfloat16 [64, 16384], P(None, 'fsdp'), may hold values from -0.75 to 0.75
Outputs:
- latent_gradient: bfloat16 [8192, 512], P(('dp', 'fsdp'))
- grad_a: float32 [512, 64], replicated
- grad_b: float32 [64, 16384], P(None, 'fsdp')
The draws below stay inside these ranges and needn't reach their ends.
All inputs are finite; a program needn't handle non-finite values.
Results may differ from the reference program's by a relative error of at most 0.0049.
Values may be sent and summed in bfloat16 or wider, within the bound.
No kernel may reach another device: no remote copies, remote signals or barrier semaphores. Data moves between devices by JAX's collectives and lax.ppermute only.
A program may use at most 128 MiB of HBM per device.

```python
import math
import jax
import jax.numpy as jnp

LATENT_WIDTH = 512
ADAPTER_RANK = 64
BLOCK = 128
OUTPUT_COLUMNS = 16384
TOKENS = 8192


def strengthened(result, own_key, source, target, shards_of, factor):
    owner, partner = [(jnp.arange(result.shape[axis_at]) // (result.shape[axis_at] // shards_of)).reshape([-1 if axis == axis_at else 1 for axis in range(result.ndim)]) for axis_at in (source, target)]
    chosen = jax.random.permutation(own_key, shards_of)[partner]
    strong = (owner == chosen) | (owner == (partner + shards_of // 2) % shards_of)
    return jnp.where(strong, factor * result, result)


def steps_of(stream_key, shape, shards, low, top_value):
    def one(position, shards_of):
        heights = jax.random.uniform(jax.random.fold_in(jax.random.fold_in(stream_key, 6), position), (shards_of,), jnp.float32, low / len(shards), top_value / len(shards))
        return jnp.repeat(jnp.exp(heights), shape[position] // shards_of).reshape((-1,) + (1,) * (len(shape) - position - 1))

    gain = one(*shards[0])
    for cut in shards[1:]:
        gain = gain * one(*cut)
    return gain


def centred(stream_key, dims, deviation, limit, pieces=(), kind=jnp.bfloat16):
    loudness = steps_of(stream_key, dims, pieces, -0.22, 0.18) if pieces else 1.0
    drawn = jax.random.normal(stream_key, dims, jnp.float32) * deviation * loudness
    return jnp.minimum(jnp.maximum(drawn, -limit), limit).astype(kind)


def bell_draw_with(rng, extent, spread, most, cuts, heavy, dtype=jnp.bfloat16):
    entries = spread * jax.random.normal(rng, extent, jnp.float32)
    if cuts:
        entries = entries * steps_of(rng, extent, cuts, -0.22, 0.18)
    return jnp.clip(strengthened(entries, jax.random.fold_in(rng, 3), *heavy), -most, most).astype(dtype)


def setup_inputs(seed: int = 0) -> dict:
    streams_of = jax.random.split(jax.random.key(seed), 7)
    return {
        "latent": centred(streams_of[0], (TOKENS, LATENT_WIDTH), 1.0, 6.0, ((0, 32),)),
        "cotangent": bell_draw_with(streams_of[1], (TOKENS, OUTPUT_COLUMNS), 0.2, 2.0, ((0, 32),), (0, 1, 32, 2.75)),
        "quant": centred(streams_of[2], (LATENT_WIDTH, OUTPUT_COLUMNS), 1.0, 6.0, ((1, 8),)),
        "scales": jnp.clip(jnp.exp(math.log(0.09) - 1.7917595 * jax.random.uniform(streams_of[3], (LATENT_WIDTH // BLOCK, OUTPUT_COLUMNS // BLOCK), jnp.float32) ** steps_of(streams_of[3], (LATENT_WIDTH // BLOCK, OUTPUT_COLUMNS // BLOCK), ((1, 8),), -0.2, 0.2)), 0.015, 0.09),
        "adapter_down": centred(streams_of[4], (LATENT_WIDTH, ADAPTER_RANK), LATENT_WIDTH ** -0.5, 0.25),
        "adapter_up": centred(streams_of[5], (ADAPTER_RANK, OUTPUT_COLUMNS), ADAPTER_RANK ** -0.5, 0.75, ((1, 8),)),
    }


def expand(scales):
    return jnp.repeat(jnp.repeat(scales, BLOCK, axis=0), BLOCK, axis=1)

def reference(latent, cotangent, quant, scales, adapter_down, adapter_up):
    weight = (quant.astype(jnp.float32) * expand(scales)).astype(jnp.bfloat16)
    lowrank_term = jnp.dot(latent, adapter_down, preferred_element_type=jnp.float32).astype(jnp.bfloat16)
    adapter_pass = jnp.dot(cotangent, adapter_up.T, preferred_element_type=jnp.float32).astype(jnp.bfloat16)
    frozen_term = jnp.dot(cotangent, weight.T, preferred_element_type=jnp.float32)
    latent_gradient = (frozen_term + jnp.dot(adapter_pass, adapter_down.T, preferred_element_type=jnp.float32)).astype(jnp.bfloat16)
    factor = 1.0 / jnp.sqrt(jnp.float32(TOKENS))
    grad_a = jnp.dot(latent.T, adapter_pass, preferred_element_type=jnp.float32) * factor
    grad_b = jnp.dot(lowrank_term.T, cotangent, preferred_element_type=jnp.float32) * factor
    return (latent_gradient, grad_a, grad_b)
```

```python
import jax
import jax.numpy as jnp
import numpy as np
from jax import lax
from jax.experimental import pallas as pl
from jax.experimental.pallas import tpu as pltpu
from jax.sharding import PartitionSpec as P

BLOCK = 128
F32 = jnp.float32
BF16 = jnp.bfloat16
MIB = 1 << 20
VMEM_MIB = 50


def nt(left, right):
    return lax.dot_general(left, right, (((1,), (1,)), ((), ())), preferred_element_type=F32)


def nn(left, right):
    return jnp.dot(left, right, preferred_element_type=F32)


def tn(left, right):
    return lax.dot_general(left, right, (((0,), (0,)), ((), ())), preferred_element_type=F32)


def params(mib):
    return pltpu.CompilerParams(vmem_limit_bytes=mib * MIB)


def cost(flops, nbytes):
    return pl.CostEstimate(flops=flops, bytes_accessed=nbytes, transcendentals=0)


def together(*arrays):
    return lax.optimization_barrier(arrays)


def assemble(*outputs):
    pieces = [piece for output in outputs for piece in output]
    where = [
        (at, sum(count for _, _, count in output[:k]))
        for at, output in enumerate(outputs)
        for k in range(len(output))
    ]

    def body(*refs):
        ins, outs, semaphore = refs[: len(pieces)], refs[len(pieces) : -1], refs[-1]
        copies = [
            pltpu.make_async_copy(
                ins[k].at[pl.ds(start, count)], outs[to].at[pl.ds(row, count)], semaphore.at[k]
            )
            for k, ((_, start, count), (to, row)) in enumerate(zip(pieces, where))
        ]
        for copy in copies:
            copy.start()
        for copy in copies:
            copy.wait()

    return pl.pallas_call(
        body,
        in_specs=[pl.BlockSpec(memory_space=pl.ANY)] * len(pieces),
        out_specs=[pl.BlockSpec(memory_space=pl.ANY)] * len(outputs),
        out_shape=[
            jax.ShapeDtypeStruct((sum(c for _, _, c in output), output[0][0].shape[1]), BF16)
            for output in outputs
        ],
        scratch_shapes=[pltpu.SemaphoreType.DMA((len(pieces),))],
        compiler_params=params(1),
        cost_estimate=cost(0, 4 * sum(c * a.shape[1] for a, _, c in pieces)),
        name="assemble",
    )(*[a for a, _, _ in pieces])


def terms_b(info, cotangent, partner, low, low_partner, n):
    tokens, columns = cotangent.shape
    part = columns // n // 2
    span = part // 2
    rank = low.shape[0]

    def body(info, mine, partner, low, low_partner, keep, send):
        x = info[1]

        def term(which):
            here = pl.ds(pl.multiple_of(which * span, BLOCK), span)
            return nn(low[...], mine[:, here]) + nn(low_partner[...], partner[:, here])

        keep[...] = term(x)
        send[...] = term(1 - x).astype(send.dtype)

    return pl.pallas_call(
        body,
        grid_spec=pltpu.PrefetchScalarGridSpec(
            num_scalar_prefetch=1,
            grid=(n,),
            in_specs=[pl.BlockSpec((tokens, part), lambda j, info: (0, 2 * info[2 + j] + info[0]))] * 2
            + [pl.BlockSpec((rank, tokens), lambda j, info: (0, 0))] * 2,
            out_specs=[pl.BlockSpec((rank, span), lambda j, info: (0, info[2 + n + j]))] * 2,
        ),
        out_shape=[
            jax.ShapeDtypeStruct((rank, n * span), F32),
            jax.ShapeDtypeStruct((rank, n * span), BF16),
        ],
        compiler_params=params(VMEM_MIB),
        cost_estimate=cost(4 * tokens * rank * n * part, tokens * n * part * 4),
        name="terms_b",
    )(info, cotangent, partner, low, low_partner)


def products(info, first, cotangent, partner, pieces, begun, n, name):
    tokens, columns = cotangent.shape
    part = columns // n // 2
    steps = len(pieces)
    arrays = [rows[0] for piece in pieces for rows in piece]
    specs = [
        pl.BlockSpec((block, part), lambda j, info, which=which: (which, 0))
        for piece in pieces
        for _, block, which, _ in piece
    ]
    width = sum(rows.stop - rows.start for _, _, _, rows in pieces[0])
    old = [] if begun is None else [begun]
    whole = pl.BlockSpec((2 * tokens, width), lambda j, info: (0, 0))

    def body(info, mine, partner, *refs):
        row_refs, old_refs, (out, weight) = refs[: len(arrays)], refs[len(arrays) : -2], refs[-2:]
        at = pl.program_id(0)

        @pl.when(at == 0)
        def _():
            out[...] = old_refs[0][...] if old_refs else jnp.zeros_like(out)

        taken = 0
        for j, piece in enumerate(pieces):

            @pl.when(at == j)
            def _(piece=piece, taken=taken):
                start = 0
                for k, (_, _, _, rows) in enumerate(piece):
                    count = rows.stop - rows.start
                    weight[pl.ds(start, count), :] = row_refs[taken + k][pl.ds(rows.start, count), :]
                    start += count
                if start < width:
                    weight[pl.ds(start, width - start), :] = jnp.zeros((width - start, part), BF16)

            taken += len(piece)

        out[:tokens, :] += nt(mine[...], weight[...])
        out[tokens:, :] += nt(partner[...], weight[...])

    return pl.pallas_call(
        body,
        grid_spec=pltpu.PrefetchScalarGridSpec(
            num_scalar_prefetch=1,
            grid=(steps,),
            in_specs=[pl.BlockSpec((tokens, part), lambda j, info: (0, 2 * info[first + j] + info[0]))]
            * 2
            + specs
            + [whole] * len(old),
            out_specs=whole,
            scratch_shapes=[pltpu.VMEM((width, part), BF16)],
        ),
        out_shape=jax.ShapeDtypeStruct((2 * tokens, width), F32),
        compiler_params=params(VMEM_MIB),
        cost_estimate=cost(
            4 * steps * tokens * width * part, steps * part * (4 * tokens + 2 * width) + 8 * tokens * width
        ),
        name=name,
    )(info, cotangent, partner, *arrays, *old)


def finish(info, mine, other, factor, part):
    rank, wide = mine.shape
    span = wide - part

    def body(info, factor, mine, other, grad_b, grad_a):
        scale = factor[0]

        def put(first, second):
            grad_b[:, :part] = first[:, :part] * scale
            grad_b[:, part:] = second[:, :part] * scale
            grad_a[:, :span] = first[:, part:] * scale
            grad_a[:, span:] = second[:, part:] * scale

        @pl.when(info[0] == 0)
        def _():
            put(mine, other)

        @pl.when(info[0] != 0)
        def _():
            put(other, mine)

    whole = pl.BlockSpec((rank, wide), lambda i, info: (0, 0))
    return pl.pallas_call(
        body,
        grid_spec=pltpu.PrefetchScalarGridSpec(
            num_scalar_prefetch=1,
            grid=(1,),
            in_specs=[pl.BlockSpec(memory_space=pltpu.SMEM), whole, whole],
            out_specs=[
                pl.BlockSpec((rank, 2 * part), lambda i, info: (0, 0)),
                pl.BlockSpec((rank, 2 * span), lambda i, info: (0, 0)),
            ],
        ),
        out_shape=[
            jax.ShapeDtypeStruct((rank, 2 * part), F32),
            jax.ShapeDtypeStruct((rank, 2 * span), F32),
        ],
        compiler_params=params(8),
        cost_estimate=cost(0, 16 * rank * wide),
        name="finish",
    )(info, factor, mine, other)


def make(mesh):
    n = mesh.shape["fsdp"]
    dp = mesh.shape["dp"]
    half = n // 2
    order = list(range(0, n, 2)) + list(range(n - 1, 0, -2))
    bits = n.bit_length() - 1

    def forward(a):
        return lax.ppermute(a, "fsdp", [(order[i], order[(i + 1) % n]) for i in range(n)])

    def backward(a):
        return lax.ppermute(a, "fsdp", [(order[(i + 1) % n], order[i]) for i in range(n)])

    def over(a, axis, bit):
        return lax.ppermute(a, axis, [(i, i ^ bit) for i in range(mesh.shape[axis])])

    def shards(latent, cotangent, quant, scales, adapter_down, adapter_up):
        tokens = cotangent.shape[0]
        width, own = quant.shape
        rank = adapter_up.shape[0]
        part = own // 2
        given = width * 3 // 8
        ring = width - given
        device = lax.axis_index("dp")
        core = device & 1
        x = (device >> 1) & 1
        me = lax.axis_index("fsdp")
        place = jnp.where(me & 1 == 0, me >> 1, n - 1 - (me >> 1))

        def shard(offset):
            spot = (place + offset + n) & (n - 1)
            return jnp.where(spot < half, 2 * spot, 2 * (n - 1 - spot) + 1)

        offsets = [s * h for h in range(1, half) for s in (-1, 1)]
        offsets = [0] + offsets[:-2] + [-half] + offsets[-2:]
        shard_of = shard(np.array(offsets, np.int32))
        flipped = sum(((shard_of >> k) & 1) << (bits - 1 - k) for k in range(bits))
        info = jnp.concatenate([jnp.stack([core, x]), shard_of, flipped]).astype(jnp.int32)

        my_quant = lax.dynamic_slice_in_dim(quant, core * part, part, 1)
        my_scales = lax.dynamic_slice_in_dim(scales, core * (part // BLOCK), part // BLOCK, 1)
        my_up = lax.dynamic_slice_in_dim(adapter_up, core * part, part, 1)
        weight = (
            my_quant.astype(F32) * jnp.repeat(jnp.repeat(my_scales, BLOCK, axis=0), BLOCK, axis=1)
        ).astype(BF16)
        shared = weight[given:ring]
        ends = (weight[:given], weight[ring:])
        chunk = jnp.concatenate([my_up, jnp.where(x == 0, ends[0], ends[1]), shared], axis=0)
        missing = jnp.where(x == 0, ends[1], ends[0])

        stay = rank + given
        cut = max(given, ring // 2)

        def give(front, rear):
            return over(jnp.concatenate([front[rank:stay], rear[rank:stay]], axis=0), "dp", 2)

        partner = over(cotangent, "dp", 1)
        latent_partner = over(latent, "dp", 1)
        chunks, gifts = {0: chunk}, {}

        span = width // 2
        halves = jnp.concatenate(
            [lax.dynamic_slice_in_dim(a, core * span, span, 1) for a in (latent, latent_partner)], axis=0
        )

        low, low_partner = [
            lax.dot_general(adapter_down, a, (((0,), (1,)), ((), ())), preferred_element_type=F32).astype(BF16)
            for a in (latent, latent_partner)
        ]
        total_b, send = terms_b(info, cotangent, partner, low, low_partner, n)
        arrived = over(send, "dp", 2)

        chunks[-1], chunks[1] = together(forward(chunk), backward(chunk), send)[:2]
        far_up = lax.ppermute(
            together(my_up, chunks[1])[0], "fsdp", [(order[i], order[(i + half) % n]) for i in range(n)]
        )
        chunks[-2], chunks[2] = forward(chunks[-1]), backward(chunks[1])

        def ups_of(hop):
            return [[(chunks[s * hop], rank, 0, range(rank))] for s in (-1, 1)]

        def product(first, pieces, begun, name):
            return products(info, 2 + first, cotangent, partner, pieces, begun, n, name)

        sums = product(0, [[(chunk, rank, 0, range(rank))]] + ups_of(1), None, "through_first")
        front, rear, arrived, sums = together(chunks[-1], chunks[1], arrived, sums)
        gifts[1] = give(front, rear)

        def rows_of(hop):
            return [
                [
                    (chunks[s * hop], rank + ring, 0, range(rank, rank + ring)),
                    (gifts[hop], given, (s + 1) // 2, range(given)),
                ]
                for s in (-1, 1)
            ]

        own = [
            (chunk, rank + ring, 0, range(rank, rank + ring)),
            (missing, given, 0, range(given)),
        ]
        def halve(total, bit):
            size = total.shape[1] // 2
            side = (me // bit) & 1
            return (
                lax.dynamic_slice_in_dim(total, (1 - side) * size, size, 1).astype(BF16),
                lax.dynamic_slice_in_dim(total, side * size, size, 1),
            )

        sent, total_b = halve(total_b + arrived.astype(F32), 1)

        done = product(0, [own] + rows_of(1), None, "first")
        for hop in range(3, half):
            chunks[-hop], chunks[hop] = forward(chunks[1 - hop]), backward(chunks[hop - 1])
            gifts[hop - 1] = give(chunks[1 - hop], chunks[hop - 1])
            if hop < half - 1:
                chunks[-hop], chunks[hop], gifts[hop - 1], done = together(
                    chunks[-hop], chunks[hop], gifts[hop - 1], done
                )
                done = product(2 * hop - 3, rows_of(hop - 1), done, "middle")

        pieces = []
        for k in range(2, half - 1):
            pieces += ups_of(k)
        pieces += [[(far_up, rank, 0, range(rank))]]
        sums = product(3, pieces, sums, "through_second")
        part_b = over(together(sent, chunks[-2])[0], "fsdp", 1)
        hop = half - 1
        chunks[-hop], chunks[hop], done, sums = together(chunks[-hop], chunks[hop], done, sums)
        gift, front, rear = assemble(
            [(chunks[k * hop], rank, given) for k in (-1, 1)],
            [(chunks[-hop], rank, cut)],
            [(chunks[hop], rank + cut, ring - cut)],
        )
        gifts[hop] = over(gift, "dp", 2)
        sums, gift = together(sums, gift)
        both_sums = product(2 * hop, ups_of(hop), sums, "through_last")
        others = over(both_sums, "dp", 1)
        part_b = together(part_b, both_sums)[0]
        swapped = jnp.concatenate([others[tokens:], others[:tokens]], axis=0)
        through = (both_sums + swapped).astype(BF16)

        total_a = tn(through, halves)
        through = through[:tokens]
        part_a = over(total_a, "fsdp", 1)
        done = product(2 * hop - 3, rows_of(hop - 1), done, "middle")

        total_a, total_b = total_a + part_a, total_b + part_b.astype(F32)
        sent, total_b = halve(total_b, 2)
        front, rear, total_a, sent, done = together(
            forward(front), backward(rear), total_a, sent, done
        )
        gifts[half] = over(front[:given], "dp", 2)
        part_a, part_b = over(total_a, "fsdp", 2), over(sent, "fsdp", 2)
        part_a, part_b, done, gifts[hop] = together(part_a, part_b, done, gifts[hop])
        total_a, total_b = total_a + part_a, total_b + part_b.astype(F32)
        done = product(2 * half - 2, rows_of(half - 1), done, "late")
        bit = 4
        while bit < n:
            total_a = total_a + over(total_a, "fsdp", bit)
            sent, total_b = halve(total_b, bit)
            total_b = total_b + over(sent, "fsdp", bit).astype(F32)
            bit *= 2
        bit = 4
        while bit < dp:
            total_a = total_a + over(total_a, "dp", bit)
            total_b = total_b + over(total_b, "dp", bit)
            bit *= 2
        total_a, total_b, gifts[half], done = together(total_a, total_b, gifts[half], done)
        totals = jnp.concatenate([total_b, total_a], axis=1)
        others = over(totals, "dp", 2)
        last = [
            (front, cut, 0, range(cut)),
            (rear, ring - cut, 0, range(ring - cut)),
            (gifts[half], given, 0, range(given)),
        ]
        done = product(2 * half - 3, [last], done, "last")
        others, swapped = together(others, over(done[tokens:], "dp", 1))
        other_b, total_a = others[:, : part // 2], total_a + others[:, part // 2 :]
        low_x, high_x = jnp.where(x == 0, total_b, other_b), jnp.where(x == 0, other_b, total_b)
        ends = jnp.concatenate([low_x, high_x, total_a], axis=1)
        other_ends = over(ends, "dp", 1)
        factor = 1.0 / jnp.sqrt(F32(tokens * dp * n))
        grad_b, grad_a = finish(info, ends, other_ends, factor.reshape(1), part)
        grad_a = grad_a.T

        frozen = done[:tokens] + swapped
        begin, middle, end = frozen[:, :given], frozen[:, given:ring], frozen[:, ring:]
        frozen = jnp.concatenate(
            [jnp.where(x == 0, begin, end), middle, jnp.where(x == 0, end, begin)], axis=1
        )
        latent_gradient = (frozen + nt(through, adapter_down)).astype(BF16)
        return (latent_gradient, grad_a, grad_b)

    return shards


def solution(mesh):
    placed = (
        P(("dp", "fsdp"), None),
        P(("dp", "fsdp"), None),
        P(None, "fsdp"),
        P(None, "fsdp"),
        P(),
        P(None, "fsdp"),
    )
    return jax.shard_map(
        make(mesh),
        mesh=mesh,
        in_specs=placed,
        out_specs=(P(("dp", "fsdp"), None), P(), P(None, "fsdp")),
        check_vma=False,
    )
```

```python
import jax
import jax.numpy as jnp
import numpy as np
from jax import lax
from jax.experimental import pallas as pl
from jax.experimental.pallas import tpu as pltpu
from jax.sharding import PartitionSpec as P

BLOCK = 128
F32 = jnp.float32
BF16 = jnp.bfloat16
MIB = 1 << 20
VMEM_MIB = 50


def nt(left, right):
    return lax.dot_general(left, right, (((1,), (1,)), ((), ())), preferred_element_type=F32)


def nn(left, right):
    return jnp.dot(left, right, preferred_element_type=F32)


def tn(left, right):
    return lax.dot_general(left, right, (((0,), (0,)), ((), ())), preferred_element_type=F32)


def params(mib):
    return pltpu.CompilerParams(vmem_limit_bytes=mib * MIB)


def cost(flops, nbytes):
    return pl.CostEstimate(flops=flops, bytes_accessed=nbytes, transcendentals=0)


def together(*arrays):
    return lax.optimization_barrier(arrays)


def assemble(*outputs):
    pieces = [piece for output in outputs for piece in output]
    where = [
        (at, sum(count for _, _, count in output[:k]))
        for at, output in enumerate(outputs)
        for k in range(len(output))
    ]

    def body(*refs):
        ins, outs, semaphore = refs[: len(pieces)], refs[len(pieces) : -1], refs[-1]
        copies = [
            pltpu.make_async_copy(
                ins[k].at[pl.ds(start, count)], outs[to].at[pl.ds(row, count)], semaphore.at[k]
            )
            for k, ((_, start, count), (to, row)) in enumerate(zip(pieces, where))
        ]
        for copy in copies:
            copy.start()
        for copy in copies:
            copy.wait()

    return pl.pallas_call(
        body,
        in_specs=[pl.BlockSpec(memory_space=pl.ANY)] * len(pieces),
        out_specs=[pl.BlockSpec(memory_space=pl.ANY)] * len(outputs),
        out_shape=[
            jax.ShapeDtypeStruct((sum(c for _, _, c in output), output[0][0].shape[1]), BF16)
            for output in outputs
        ],
        scratch_shapes=[pltpu.SemaphoreType.DMA((len(pieces),))],
        compiler_params=params(1),
        cost_estimate=cost(0, 4 * sum(c * a.shape[1] for a, _, c in pieces)),
        name="assemble",
    )(*[a for a, _, _ in pieces])


def terms_b(info, cotangent, partner, low, low_partner, n):
    tokens, columns = cotangent.shape
    part = columns // n // 2
    span = part // 2
    rank = low.shape[0]

    def body(info, mine, partner, low, low_partner, keep, send):
        x = info[1]

        def term(which):
            here = pl.ds(pl.multiple_of(which * span, BLOCK), span)
            return nn(low[...], mine[:, here]) + nn(low_partner[...], partner[:, here])

        keep[...] = term(x)
        send[...] = term(1 - x).astype(send.dtype)

    return pl.pallas_call(
        body,
        grid_spec=pltpu.PrefetchScalarGridSpec(
            num_scalar_prefetch=1,
            grid=(n,),
            in_specs=[pl.BlockSpec((tokens, part), lambda j, info: (0, 2 * info[2 + j] + info[0]))] * 2
            + [pl.BlockSpec((rank, tokens), lambda j, info: (0, 0))] * 2,
            out_specs=[pl.BlockSpec((rank, span), lambda j, info: (0, info[2 + n + j]))] * 2,
        ),
        out_shape=[
            jax.ShapeDtypeStruct((rank, n * span), F32),
            jax.ShapeDtypeStruct((rank, n * span), BF16),
        ],
        compiler_params=params(VMEM_MIB),
        cost_estimate=cost(4 * tokens * rank * n * part, tokens * n * part * 4),
        name="terms_b",
    )(info, cotangent, partner, low, low_partner)


def products(info, first, cotangent, partner, pieces, begun, n, name):
    tokens, columns = cotangent.shape
    part = columns // n // 2
    steps = len(pieces)
    arrays = [rows[0] for piece in pieces for rows in piece]
    specs = [
        pl.BlockSpec((block, part), lambda j, info, which=which: (which, 0))
        for piece in pieces
        for _, block, which, _ in piece
    ]
    width = sum(rows.stop - rows.start for _, _, _, rows in pieces[0])
    old = [] if begun is None else [begun]
    whole = pl.BlockSpec((2 * tokens, width), lambda j, info: (0, 0))

    def body(info, mine, partner, *refs):
        row_refs, old_refs, (out, weight) = refs[: len(arrays)], refs[len(arrays) : -2], refs[-2:]
        at = pl.program_id(0)

        @pl.when(at == 0)
        def _():
            out[...] = old_refs[0][...] if old_refs else jnp.zeros_like(out)

        taken = 0
        for j, piece in enumerate(pieces):

            @pl.when(at == j)
            def _(piece=piece, taken=taken):
                start = 0
                for k, (_, _, _, rows) in enumerate(piece):
                    count = rows.stop - rows.start
                    weight[pl.ds(start, count), :] = row_refs[taken + k][pl.ds(rows.start, count), :]
                    start += count
                if start < width:
                    weight[pl.ds(start, width - start), :] = jnp.zeros((width - start, part), BF16)

            taken += len(piece)

        out[:tokens, :] += nt(mine[...], weight[...])
        out[tokens:, :] += nt(partner[...], weight[...])

    return pl.pallas_call(
        body,
        grid_spec=pltpu.PrefetchScalarGridSpec(
            num_scalar_prefetch=1,
            grid=(steps,),
            in_specs=[pl.BlockSpec((tokens, part), lambda j, info: (0, 2 * info[first + j] + info[0]))]
            * 2
            + specs
            + [whole] * len(old),
            out_specs=whole,
            scratch_shapes=[pltpu.VMEM((width, part), BF16)],
        ),
        out_shape=jax.ShapeDtypeStruct((2 * tokens, width), F32),
        compiler_params=params(VMEM_MIB),
        cost_estimate=cost(
            4 * steps * tokens * width * part, steps * part * (4 * tokens + 2 * width) + 8 * tokens * width
        ),
        name=name,
    )(info, cotangent, partner, *arrays, *old)


def finish(info, mine, other, factor, part):
    rank, wide = mine.shape
    span = wide - part

    def body(info, factor, mine, other, grad_b, grad_a):
        scale = factor[0]

        def put(first, second):
            grad_b[:, :part] = first[:, :part] * scale
            grad_b[:, part:] = second[:, :part] * scale
            grad_a[:, :span] = first[:, part:] * scale
            grad_a[:, span:] = second[:, part:] * scale

        @pl.when(info[0] == 0)
        def _():
            put(mine, other)

        @pl.when(info[0] != 0)
        def _():
            put(other, mine)

    whole = pl.BlockSpec((rank, wide), lambda i, info: (0, 0))
    return pl.pallas_call(
        body,
        grid_spec=pltpu.PrefetchScalarGridSpec(
            num_scalar_prefetch=1,
            grid=(1,),
            in_specs=[pl.BlockSpec(memory_space=pltpu.SMEM), whole, whole],
            out_specs=[
                pl.BlockSpec((rank, 2 * part), lambda i, info: (0, 0)),
                pl.BlockSpec((rank, 2 * span), lambda i, info: (0, 0)),
            ],
        ),
        out_shape=[
            jax.ShapeDtypeStruct((rank, 2 * part), F32),
            jax.ShapeDtypeStruct((rank, 2 * span), F32),
        ],
        compiler_params=params(8),
        cost_estimate=cost(0, 16 * rank * wide),
        name="finish",
    )(info, factor, mine, other)


def make(mesh):
    n = mesh.shape["fsdp"]
    dp = mesh.shape["dp"]
    half = n // 2
    order = list(range(0, n, 2)) + list(range(n - 1, 0, -2))
    bits = n.bit_length() - 1

    def forward(a):
        return lax.ppermute(a, "fsdp", [(order[i], order[(i + 1) % n]) for i in range(n)])

    def backward(a):
        return lax.ppermute(a, "fsdp", [(order[(i + 1) % n], order[i]) for i in range(n)])

    def over(a, axis, bit):
        return lax.ppermute(a, axis, [(i, i ^ bit) for i in range(mesh.shape[axis])])

    def shards(latent, cotangent, quant, scales, adapter_down, adapter_up):
        tokens = cotangent.shape[0]
        width, own = quant.shape
        rank = adapter_up.shape[0]
        part = own // 2
        given = width * 3 // 8
        ring = width - given
        device = lax.axis_index("dp")
        core = device & 1
        x = (device >> 1) & 1
        me = lax.axis_index("fsdp")
        place = jnp.where(me & 1 == 0, me >> 1, n - 1 - (me >> 1))

        def shard(offset):
            spot = (place + offset + n) & (n - 1)
            return jnp.where(spot < half, 2 * spot, 2 * (n - 1 - spot) + 1)

        offsets = [s * h for h in range(1, half) for s in (-1, 1)]
        offsets = [0] + offsets[:-2] + [-half] + offsets[-2:]
        shard_of = shard(np.array(offsets, np.int32))
        flipped = sum(((shard_of >> k) & 1) << (bits - 1 - k) for k in range(bits))
        info = jnp.concatenate([jnp.stack([core, x]), shard_of, flipped]).astype(jnp.int32)

        my_quant = lax.dynamic_slice_in_dim(quant, core * part, part, 1)
        my_scales = lax.dynamic_slice_in_dim(scales, core * (part // BLOCK), part // BLOCK, 1)
        my_up = lax.dynamic_slice_in_dim(adapter_up, core * part, part, 1)
        weight = (
            my_quant.astype(F32) * jnp.repeat(jnp.repeat(my_scales, BLOCK, axis=0), BLOCK, axis=1)
        ).astype(BF16)
        shared = weight[given:ring]
        ends = (weight[:given], weight[ring:])
        chunk = jnp.concatenate([my_up, jnp.where(x == 0, ends[0], ends[1]), shared], axis=0)
        missing = jnp.where(x == 0, ends[1], ends[0])

        stay = rank + given
        cut = max(given, ring // 2)

        def give(front, rear):
            return over(jnp.concatenate([front[rank:stay], rear[rank:stay]], axis=0), "dp", 2)

        partner = over(cotangent, "dp", 1)
        latent_partner = over(latent, "dp", 1)
        chunks, gifts = {0: chunk}, {}

        span = width // 2
        halves = jnp.concatenate(
            [lax.dynamic_slice_in_dim(a, core * span, span, 1) for a in (latent, latent_partner)], axis=0
        )

        low, low_partner = [
            lax.dot_general(adapter_down, a, (((0,), (1,)), ((), ())), preferred_element_type=F32).astype(BF16)
            for a in (latent, latent_partner)
        ]
        total_b, send = terms_b(info, cotangent, partner, low, low_partner, n)
        arrived = over(send, "dp", 2)

        chunks[-1], chunks[1] = together(forward(chunk), backward(chunk), send)[:2]
        far_up = lax.ppermute(
            together(my_up, chunks[1])[0], "fsdp", [(order[i], order[(i + half) % n]) for i in range(n)]
        )
        chunks[-2], chunks[2] = forward(chunks[-1]), backward(chunks[1])

        def ups_of(hop):
            return [[(chunks[s * hop], rank, 0, range(rank))] for s in (-1, 1)]

        def product(first, pieces, begun, name):
            return products(info, 2 + first, cotangent, partner, pieces, begun, n, name)

        sums = product(0, [[(chunk, rank, 0, range(rank))]] + ups_of(1), None, "through_first")
        front, rear, arrived, sums = together(chunks[-1], chunks[1], arrived, sums)
        gifts[1] = give(front, rear)

        def rows_of(hop):
            return [
                [
                    (chunks[s * hop], rank + ring, 0, range(rank, rank + ring)),
                    (gifts[hop], given, (s + 1) // 2, range(given)),
                ]
                for s in (-1, 1)
            ]

        own = [
            (chunk, rank + ring, 0, range(rank, rank + ring)),
            (missing, given, 0, range(given)),
        ]
        def halve(total, bit):
            size = total.shape[1] // 2
            side = (me // bit) & 1
            return (
                lax.dynamic_slice_in_dim(total, (1 - side) * size, size, 1).astype(BF16),
                lax.dynamic_slice_in_dim(total, side * size, size, 1),
            )

        sent, total_b = halve(total_b + arrived.astype(F32), 1)

        done = product(0, [own] + rows_of(1), None, "first")
        for hop in range(3, half):
            chunks[-hop], chunks[hop] = forward(chunks[1 - hop]), backward(chunks[hop - 1])
            gifts[hop - 1] = give(chunks[1 - hop], chunks[hop - 1])
            if hop < half - 1:
                chunks[-hop], chunks[hop], gifts[hop - 1], done = together(
                    chunks[-hop], chunks[hop], gifts[hop - 1], done
                )
                done = product(2 * hop - 3, rows_of(hop - 1), done, "middle")

        pieces = []
        for k in range(2, half - 1):
            pieces += ups_of(k)
        pieces += [[(far_up, rank, 0, range(rank))]]
        sums = product(3, pieces, sums, "through_second")
        part_b = over(together(sent, chunks[-2])[0], "fsdp", 1)
        hop = half - 1
        chunks[-hop], chunks[hop], done, sums = together(chunks[-hop], chunks[hop], done, sums)
        gift, front, rear = assemble(
            [(chunks[k * hop], rank, given) for k in (-1, 1)],
            [(chunks[-hop], rank, cut)],
            [(chunks[hop], rank + cut, ring - cut)],
        )
        gifts[hop] = over(gift, "dp", 2)
        sums, gift = together(sums, gift)
        both_sums = product(2 * hop, ups_of(hop), sums, "through_last")
        others = over(both_sums, "dp", 1)
        part_b = together(part_b, both_sums)[0]
        swapped = jnp.concatenate([others[tokens:], others[:tokens]], axis=0)
        through = (both_sums + swapped).astype(BF16)

        total_a = tn(through, halves)
        through = through[:tokens]
        part_a = over(total_a, "fsdp", 1)
        done = product(2 * hop - 3, rows_of(hop - 1), done, "middle")

        total_a, total_b = total_a + part_a, total_b + part_b.astype(F32)
        sent, total_b = halve(total_b, 2)
        front, rear, total_a, sent, done = together(
            forward(front), backward(rear), total_a, sent, done
        )
        gifts[half] = over(front[:given], "dp", 2)
        part_a, part_b = over(total_a, "fsdp", 2), over(sent, "fsdp", 2)
        part_a, part_b, done, gifts[hop] = together(part_a, part_b, done, gifts[hop])
        total_a, total_b = total_a + part_a, total_b + part_b.astype(F32)
        done = product(2 * half - 2, rows_of(half - 1), done, "late")
        bit = 4
        while bit < n:
            total_a = total_a + over(total_a, "fsdp", bit)
            sent, total_b = halve(total_b, bit)
            total_b = total_b + over(sent, "fsdp", bit).astype(F32)
            bit *= 2
        bit = 4
        while bit < dp:
            total_a = total_a + over(total_a, "dp", bit)
            total_b = total_b + over(total_b, "dp", bit)
            bit *= 2
        total_a, total_b, gifts[half], done = together(total_a, total_b, gifts[half], done)
        totals = jnp.concatenate([total_b, total_a], axis=1)
        others = over(totals, "dp", 2)
        last = [
            (front, cut, 0, range(cut)),
            (rear, ring - cut, 0, range(ring - cut)),
            (gifts[half], given, 0, range(given)),
        ]
        done = product(2 * half - 3, [last], done, "last")
        others, done = together(others, done)
        other_b, total_a = others[:, : part // 2], total_a + others[:, part // 2 :]
        low_x, high_x = jnp.where(x == 0, total_b, other_b), jnp.where(x == 0, other_b, total_b)
        ends = jnp.concatenate([low_x, high_x, total_a], axis=1)
        other_ends = over(ends, "dp", 1)
        factor = 1.0 / jnp.sqrt(F32(tokens * dp * n))
        grad_b, grad_a = finish(info, ends, other_ends, factor.reshape(1), part)
        grad_a = grad_a.T

        frozen = done[:tokens] + over(done[tokens:], "dp", 1)
        begin, middle, end = frozen[:, :given], frozen[:, given:ring], frozen[:, ring:]
        frozen = jnp.concatenate(
            [jnp.where(x == 0, begin, end), middle, jnp.where(x == 0, end, begin)], axis=1
        )
        latent_gradient = (frozen + nt(through, adapter_down)).astype(BF16)
        return (latent_gradient, grad_a, grad_b)

    return shards


def solution(mesh):
    placed = (
        P(("dp", "fsdp"), None),
        P(("dp", "fsdp"), None),
        P(None, "fsdp"),
        P(None, "fsdp"),
        P(),
        P(None, "fsdp"),
    )
    return jax.shard_map(
        make(mesh),
        mesh=mesh,
        in_specs=placed,
        out_specs=(P(("dp", "fsdp"), None), P(), P(None, "fsdp")),
        check_vma=False,
    )
```

```python
import jax
import jax.numpy as jnp
import numpy as np
from jax import lax
from jax.experimental import pallas as pl
from jax.experimental.pallas import tpu as pltpu
from jax.sharding import PartitionSpec as P

BLOCK = 128
F32 = jnp.float32
BF16 = jnp.bfloat16
MIB = 1 << 20
VMEM_MIB = 50


def nt(left, right):
    return lax.dot_general(left, right, (((1,), (1,)), ((), ())), preferred_element_type=F32)


def nn(left, right):
    return jnp.dot(left, right, preferred_element_type=F32)


def tn(left, right):
    return lax.dot_general(left, right, (((0,), (0,)), ((), ())), preferred_element_type=F32)


def params(mib):
    return pltpu.CompilerParams(vmem_limit_bytes=mib * MIB)


def cost(flops, nbytes):
    return pl.CostEstimate(flops=flops, bytes_accessed=nbytes, transcendentals=0)


def together(*arrays):
    return lax.optimization_barrier(arrays)


def assemble(*outputs):
    pieces = [piece for output in outputs for piece in output]
    where = [
        (at, sum(count for _, _, count in output[:k]))
        for at, output in enumerate(outputs)
        for k in range(len(output))
    ]

    def body(*refs):
        ins, outs, semaphore = refs[: len(pieces)], refs[len(pieces) : -1], refs[-1]
        copies = [
            pltpu.make_async_copy(
                ins[k].at[pl.ds(start, count)], outs[to].at[pl.ds(row, count)], semaphore.at[k]
            )
            for k, ((_, start, count), (to, row)) in enumerate(zip(pieces, where))
        ]
        for copy in copies:
            copy.start()
        for copy in copies:
            copy.wait()

    return pl.pallas_call(
        body,
        in_specs=[pl.BlockSpec(memory_space=pl.ANY)] * len(pieces),
        out_specs=[pl.BlockSpec(memory_space=pl.ANY)] * len(outputs),
        out_shape=[
            jax.ShapeDtypeStruct((sum(c for _, _, c in output), output[0][0].shape[1]), BF16)
            for output in outputs
        ],
        scratch_shapes=[pltpu.SemaphoreType.DMA((len(pieces),))],
        compiler_params=params(1),
        cost_estimate=cost(0, 4 * sum(c * a.shape[1] for a, _, c in pieces)),
        name="assemble",
    )(*[a for a, _, _ in pieces])


def terms_b(info, cotangent, partner, low, low_partner, n):
    tokens, columns = cotangent.shape
    part = columns // n // 2
    span = part // 2
    rank = low.shape[0]

    def body(info, mine, partner, low, low_partner, keep, send):
        x = info[1]

        def term(which):
            here = pl.ds(pl.multiple_of(which * span, BLOCK), span)
            return nn(low[...], mine[:, here]) + nn(low_partner[...], partner[:, here])

        keep[...] = term(x)
        send[...] = term(1 - x).astype(send.dtype)

    return pl.pallas_call(
        body,
        grid_spec=pltpu.PrefetchScalarGridSpec(
            num_scalar_prefetch=1,
            grid=(n,),
            in_specs=[pl.BlockSpec((tokens, part), lambda j, info: (0, 2 * info[2 + j] + info[0]))] * 2
            + [pl.BlockSpec((rank, tokens), lambda j, info: (0, 0))] * 2,
            out_specs=[pl.BlockSpec((rank, span), lambda j, info: (0, info[2 + n + j]))] * 2,
        ),
        out_shape=[
            jax.ShapeDtypeStruct((rank, n * span), F32),
            jax.ShapeDtypeStruct((rank, n * span), BF16),
        ],
        compiler_params=params(VMEM_MIB),
        cost_estimate=cost(4 * tokens * rank * n * part, tokens * n * part * 4),
        name="terms_b",
    )(info, cotangent, partner, low, low_partner)


def products(info, first, cotangent, partner, pieces, begun, n, name):
    tokens, columns = cotangent.shape
    part = columns // n // 2
    steps = len(pieces)
    arrays = [rows[0] for piece in pieces for rows in piece]
    specs = [
        pl.BlockSpec((block, part), lambda j, info, which=which: (which, 0))
        for piece in pieces
        for _, block, which, _ in piece
    ]
    width = sum(rows.stop - rows.start for _, _, _, rows in pieces[0])
    old = [] if begun is None else [begun]
    whole = pl.BlockSpec((2 * tokens, width), lambda j, info: (0, 0))

    def body(info, mine, partner, *refs):
        row_refs, old_refs, (out, weight) = refs[: len(arrays)], refs[len(arrays) : -2], refs[-2:]
        at = pl.program_id(0)

        @pl.when(at == 0)
        def _():
            out[...] = old_refs[0][...] if old_refs else jnp.zeros_like(out)

        taken = 0
        for j, piece in enumerate(pieces):

            @pl.when(at == j)
            def _(piece=piece, taken=taken):
                start = 0
                for k, (_, _, _, rows) in enumerate(piece):
                    count = rows.stop - rows.start
                    weight[pl.ds(start, count), :] = row_refs[taken + k][pl.ds(rows.start, count), :]
                    start += count
                if start < width:
                    weight[pl.ds(start, width - start), :] = jnp.zeros((width - start, part), BF16)

            taken += len(piece)

        out[:tokens, :] += nt(mine[...], weight[...])
        out[tokens:, :] += nt(partner[...], weight[...])

    return pl.pallas_call(
        body,
        grid_spec=pltpu.PrefetchScalarGridSpec(
            num_scalar_prefetch=1,
            grid=(steps,),
            in_specs=[pl.BlockSpec((tokens, part), lambda j, info: (0, 2 * info[first + j] + info[0]))]
            * 2
            + specs
            + [whole] * len(old),
            out_specs=whole,
            scratch_shapes=[pltpu.VMEM((width, part), BF16)],
        ),
        out_shape=jax.ShapeDtypeStruct((2 * tokens, width), F32),
        compiler_params=params(VMEM_MIB),
        cost_estimate=cost(
            4 * steps * tokens * width * part, steps * part * (4 * tokens + 2 * width) + 8 * tokens * width
        ),
        name=name,
    )(info, cotangent, partner, *arrays, *old)


def finish(info, mine, other, factor, part):
    rank, wide = mine.shape
    span = wide - part

    def body(info, factor, mine, other, grad_b, grad_a):
        scale = factor[0]

        def put(first, second):
            grad_b[:, :part] = first[:, :part] * scale
            grad_b[:, part:] = second[:, :part] * scale
            grad_a[:, :span] = first[:, part:] * scale
            grad_a[:, span:] = second[:, part:] * scale

        @pl.when(info[0] == 0)
        def _():
            put(mine, other)

        @pl.when(info[0] != 0)
        def _():
            put(other, mine)

    whole = pl.BlockSpec((rank, wide), lambda i, info: (0, 0))
    return pl.pallas_call(
        body,
        grid_spec=pltpu.PrefetchScalarGridSpec(
            num_scalar_prefetch=1,
            grid=(1,),
            in_specs=[pl.BlockSpec(memory_space=pltpu.SMEM), whole, whole],
            out_specs=[
                pl.BlockSpec((rank, 2 * part), lambda i, info: (0, 0)),
                pl.BlockSpec((rank, 2 * span), lambda i, info: (0, 0)),
            ],
        ),
        out_shape=[
            jax.ShapeDtypeStruct((rank, 2 * part), F32),
            jax.ShapeDtypeStruct((rank, 2 * span), F32),
        ],
        compiler_params=params(8),
        cost_estimate=cost(0, 16 * rank * wide),
        name="finish",
    )(info, factor, mine, other)


def make(mesh):
    n = mesh.shape["fsdp"]
    dp = mesh.shape["dp"]
    half = n // 2
    order = list(range(0, n, 2)) + list(range(n - 1, 0, -2))
    bits = n.bit_length() - 1

    def forward(a):
        return lax.ppermute(a, "fsdp", [(order[i], order[(i + 1) % n]) for i in range(n)])

    def backward(a):
        return lax.ppermute(a, "fsdp", [(order[(i + 1) % n], order[i]) for i in range(n)])

    def over(a, axis, bit):
        return lax.ppermute(a, axis, [(i, i ^ bit) for i in range(mesh.shape[axis])])

    def shards(latent, cotangent, quant, scales, adapter_down, adapter_up):
        tokens = cotangent.shape[0]
        width, own = quant.shape
        rank = adapter_up.shape[0]
        part = own // 2
        given = width * 11 // 32
        ring = width - given
        device = lax.axis_index("dp")
        core = device & 1
        x = (device >> 1) & 1
        me = lax.axis_index("fsdp")
        place = jnp.where(me & 1 == 0, me >> 1, n - 1 - (me >> 1))

        def shard(offset):
            spot = (place + offset + n) & (n - 1)
            return jnp.where(spot < half, 2 * spot, 2 * (n - 1 - spot) + 1)

        offsets = [s * h for h in range(1, half) for s in (-1, 1)]
        offsets = [0] + offsets[:-2] + [-half] + offsets[-2:]
        shard_of = shard(np.array(offsets, np.int32))
        flipped = sum(((shard_of >> k) & 1) << (bits - 1 - k) for k in range(bits))
        info = jnp.concatenate([jnp.stack([core, x]), shard_of, flipped]).astype(jnp.int32)

        my_quant = lax.dynamic_slice_in_dim(quant, core * part, part, 1)
        my_scales = lax.dynamic_slice_in_dim(scales, core * (part // BLOCK), part // BLOCK, 1)
        my_up = lax.dynamic_slice_in_dim(adapter_up, core * part, part, 1)
        weight = (
            my_quant.astype(F32) * jnp.repeat(jnp.repeat(my_scales, BLOCK, axis=0), BLOCK, axis=1)
        ).astype(BF16)
        shared = weight[given:ring]
        ends = (weight[:given], weight[ring:])
        chunk = jnp.concatenate([my_up, jnp.where(x == 0, ends[0], ends[1]), shared], axis=0)
        missing = jnp.where(x == 0, ends[1], ends[0])

        stay = rank + given
        cut = max(given, ring // 2)

        def give(front, rear):
            return over(jnp.concatenate([front[rank:stay], rear[rank:stay]], axis=0), "dp", 2)

        partner = over(cotangent, "dp", 1)
        latent_partner = over(latent, "dp", 1)
        chunks, gifts = {0: chunk}, {}

        span = width // 2
        halves = jnp.concatenate(
            [lax.dynamic_slice_in_dim(a, core * span, span, 1) for a in (latent, latent_partner)], axis=0
        )

        low, low_partner = [
            lax.dot_general(adapter_down, a, (((0,), (1,)), ((), ())), preferred_element_type=F32).astype(BF16)
            for a in (latent, latent_partner)
        ]
        total_b, send = terms_b(info, cotangent, partner, low, low_partner, n)
        arrived = over(send, "dp", 2)

        chunks[-1], chunks[1] = together(forward(chunk), backward(chunk), send)[:2]
        far_up = lax.ppermute(
            together(my_up, chunks[1])[0], "fsdp", [(order[i], order[(i + half) % n]) for i in range(n)]
        )
        chunks[-2], chunks[2] = forward(chunks[-1]), backward(chunks[1])

        def ups_of(hop):
            return [[(chunks[s * hop], rank, 0, range(rank))] for s in (-1, 1)]

        def product(first, pieces, begun, name):
            return products(info, 2 + first, cotangent, partner, pieces, begun, n, name)

        sums = product(0, [[(chunk, rank, 0, range(rank))]] + ups_of(1), None, "through_first")
        front, rear, arrived, sums = together(chunks[-1], chunks[1], arrived, sums)
        gifts[1] = give(front, rear)

        def rows_of(hop):
            return [
                [
                    (chunks[s * hop], rank + ring, 0, range(rank, rank + ring)),
                    (gifts[hop], given, (s + 1) // 2, range(given)),
                ]
                for s in (-1, 1)
            ]

        own = [
            (chunk, rank + ring, 0, range(rank, rank + ring)),
            (missing, given, 0, range(given)),
        ]
        def halve(total, bit):
            size = total.shape[1] // 2
            side = (me // bit) & 1
            return (
                lax.dynamic_slice_in_dim(total, (1 - side) * size, size, 1).astype(BF16),
                lax.dynamic_slice_in_dim(total, side * size, size, 1),
            )

        sent, total_b = halve(total_b + arrived.astype(F32), 1)

        done = product(0, [own] + rows_of(1), None, "first")
        for hop in range(3, half):
            chunks[-hop], chunks[hop] = forward(chunks[1 - hop]), backward(chunks[hop - 1])
            gifts[hop - 1] = give(chunks[1 - hop], chunks[hop - 1])
            if hop < half - 1:
                chunks[-hop], chunks[hop], gifts[hop - 1], done = together(
                    chunks[-hop], chunks[hop], gifts[hop - 1], done
                )
                done = product(2 * hop - 3, rows_of(hop - 1), done, "middle")

        pieces = []
        for k in range(2, half - 1):
            pieces += ups_of(k)
        pieces += [[(far_up, rank, 0, range(rank))]]
        sums = product(3, pieces, sums, "through_second")
        part_b = over(together(sent, chunks[-2])[0], "fsdp", 1)
        hop = half - 1
        chunks[-hop], chunks[hop], done, sums = together(chunks[-hop], chunks[hop], done, sums)
        gift, front, rear = assemble(
            [(chunks[k * hop], rank, given) for k in (-1, 1)],
            [(chunks[-hop], rank, cut)],
            [(chunks[hop], rank + cut, ring - cut)],
        )
        gifts[hop] = over(gift, "dp", 2)
        sums, gift = together(sums, gift)
        both_sums = product(2 * hop, ups_of(hop), sums, "through_last")
        others = over(both_sums, "dp", 1)
        part_b = together(part_b, both_sums)[0]
        swapped = jnp.concatenate([others[tokens:], others[:tokens]], axis=0)
        through = (both_sums + swapped).astype(BF16)

        total_a = tn(through, halves)
        through = through[:tokens]
        part_a = over(total_a, "fsdp", 1)
        done = product(2 * hop - 3, rows_of(hop - 1), done, "middle")

        total_a, total_b = total_a + part_a, total_b + part_b.astype(F32)
        sent, total_b = halve(total_b, 2)
        front, rear, total_a, sent, done = together(
            forward(front), backward(rear), total_a, sent, done
        )
        gifts[half] = over(front[:given], "dp", 2)
        part_a, part_b = over(total_a, "fsdp", 2), over(sent, "fsdp", 2)
        part_a, part_b, done, gifts[hop] = together(part_a, part_b, done, gifts[hop])
        total_a, total_b = total_a + part_a, total_b + part_b.astype(F32)
        done = product(2 * half - 2, rows_of(half - 1), done, "late")
        bit = 4
        while bit < n:
            total_a = total_a + over(total_a, "fsdp", bit)
            sent, total_b = halve(total_b, bit)
            total_b = total_b + over(sent, "fsdp", bit).astype(F32)
            bit *= 2
        bit = 4
        while bit < dp:
            total_a = total_a + over(total_a, "dp", bit)
            total_b = total_b + over(total_b, "dp", bit)
            bit *= 2
        total_a, total_b, gifts[half], done = together(total_a, total_b, gifts[half], done)
        totals = jnp.concatenate([total_b, total_a], axis=1)
        others = over(totals, "dp", 2)
        last = [
            (front, cut, 0, range(cut)),
            (rear, ring - cut, 0, range(ring - cut)),
            (gifts[half], given, 0, range(given)),
        ]
        done = product(2 * half - 3, [last], done, "last")
        others, done = together(others, done)
        other_b, total_a = others[:, : part // 2], total_a + others[:, part // 2 :]
        low_x, high_x = jnp.where(x == 0, total_b, other_b), jnp.where(x == 0, other_b, total_b)
        ends = jnp.concatenate([low_x, high_x, total_a], axis=1)
        other_ends = over(ends, "dp", 1)
        factor = 1.0 / jnp.sqrt(F32(tokens * dp * n))
        grad_b, grad_a = finish(info, ends, other_ends, factor.reshape(1), part)
        grad_a = grad_a.T

        frozen = done[:tokens] + over(done[tokens:], "dp", 1)
        begin, middle, end = frozen[:, :given], frozen[:, given:ring], frozen[:, ring:]
        frozen = jnp.concatenate(
            [jnp.where(x == 0, begin, end), middle, jnp.where(x == 0, end, begin)], axis=1
        )
        latent_gradient = (frozen + nt(through, adapter_down)).astype(BF16)
        return (latent_gradient, grad_a, grad_b)

    return shards


def solution(mesh):
    placed = (
        P(("dp", "fsdp"), None),
        P(("dp", "fsdp"), None),
        P(None, "fsdp"),
        P(None, "fsdp"),
        P(),
        P(None, "fsdp"),
    )
    return jax.shard_map(
        make(mesh),
        mesh=mesh,
        in_specs=placed,
        out_specs=(P(("dp", "fsdp"), None), P(), P(None, "fsdp")),
        check_vma=False,
    )
```

```python
import jax
import jax.numpy as jnp
import numpy as np
from jax import lax
from jax.experimental import pallas as pl
from jax.experimental.pallas import tpu as pltpu
from jax.sharding import PartitionSpec as P

BLOCK = 128
F32 = jnp.float32
BF16 = jnp.bfloat16
MIB = 1 << 20
VMEM_MIB = 50


def nt(left, right):
    return lax.dot_general(left, right, (((1,), (1,)), ((), ())), preferred_element_type=F32)


def nn(left, right):
    return jnp.dot(left, right, preferred_element_type=F32)


def tn(left, right):
    return lax.dot_general(left, right, (((0,), (0,)), ((), ())), preferred_element_type=F32)


def params(mib):
    return pltpu.CompilerParams(vmem_limit_bytes=mib * MIB)


def cost(flops, nbytes):
    return pl.CostEstimate(flops=flops, bytes_accessed=nbytes, transcendentals=0)


def together(*arrays):
    return lax.optimization_barrier(arrays)


def assemble(*outputs):
    pieces = [piece for output in outputs for piece in output]
    where = [
        (at, sum(count for _, _, count in output[:k]))
        for at, output in enumerate(outputs)
        for k in range(len(output))
    ]

    def body(*refs):
        ins, outs, semaphore = refs[: len(pieces)], refs[len(pieces) : -1], refs[-1]
        copies = [
            pltpu.make_async_copy(
                ins[k].at[pl.ds(start, count)], outs[to].at[pl.ds(row, count)], semaphore.at[k]
            )
            for k, ((_, start, count), (to, row)) in enumerate(zip(pieces, where))
        ]
        for copy in copies:
            copy.start()
        for copy in copies:
            copy.wait()

    return pl.pallas_call(
        body,
        in_specs=[pl.BlockSpec(memory_space=pl.ANY)] * len(pieces),
        out_specs=[pl.BlockSpec(memory_space=pl.ANY)] * len(outputs),
        out_shape=[
            jax.ShapeDtypeStruct((sum(c for _, _, c in output), output[0][0].shape[1]), BF16)
            for output in outputs
        ],
        scratch_shapes=[pltpu.SemaphoreType.DMA((len(pieces),))],
        compiler_params=params(1),
        cost_estimate=cost(0, 4 * sum(c * a.shape[1] for a, _, c in pieces)),
        name="assemble",
    )(*[a for a, _, _ in pieces])


def terms_b(info, cotangent, partner, low, low_partner, n):
    tokens, columns = cotangent.shape
    part = columns // n // 2
    span = part // 2
    rank = low.shape[0]

    def body(info, mine, partner, low, low_partner, keep, send):
        x = info[1]

        def term(which):
            here = pl.ds(pl.multiple_of(which * span, BLOCK), span)
            return nn(low[...], mine[:, here]) + nn(low_partner[...], partner[:, here])

        keep[...] = term(x)
        send[...] = term(1 - x).astype(send.dtype)

    return pl.pallas_call(
        body,
        grid_spec=pltpu.PrefetchScalarGridSpec(
            num_scalar_prefetch=1,
            grid=(n,),
            in_specs=[pl.BlockSpec((tokens, part), lambda j, info: (0, 2 * info[2 + j] + info[0]))] * 2
            + [pl.BlockSpec((rank, tokens), lambda j, info: (0, 0))] * 2,
            out_specs=[pl.BlockSpec((rank, span), lambda j, info: (0, info[2 + n + j]))] * 2,
        ),
        out_shape=[
            jax.ShapeDtypeStruct((rank, n * span), F32),
            jax.ShapeDtypeStruct((rank, n * span), BF16),
        ],
        compiler_params=params(VMEM_MIB),
        cost_estimate=cost(4 * tokens * rank * n * part, tokens * n * part * 4),
        name="terms_b",
    )(info, cotangent, partner, low, low_partner)


def products(info, first, cotangent, partner, pieces, begun, n, name):
    tokens, columns = cotangent.shape
    part = columns // n // 2
    steps = len(pieces)
    arrays = [rows[0] for piece in pieces for rows in piece]
    specs = [
        pl.BlockSpec((block, part), lambda j, info, which=which: (which, 0))
        for piece in pieces
        for _, block, which, _ in piece
    ]
    width = sum(rows.stop - rows.start for _, _, _, rows in pieces[0])
    old = [] if begun is None else [begun]
    whole = pl.BlockSpec((2 * tokens, width), lambda j, info: (0, 0))

    def body(info, mine, partner, *refs):
        row_refs, old_refs, (out, weight) = refs[: len(arrays)], refs[len(arrays) : -2], refs[-2:]
        at = pl.program_id(0)

        @pl.when(at == 0)
        def _():
            out[...] = old_refs[0][...] if old_refs else jnp.zeros_like(out)

        taken = 0
        for j, piece in enumerate(pieces):

            @pl.when(at == j)
            def _(piece=piece, taken=taken):
                start = 0
                for k, (_, _, _, rows) in enumerate(piece):
                    count = rows.stop - rows.start
                    weight[pl.ds(start, count), :] = row_refs[taken + k][pl.ds(rows.start, count), :]
                    start += count
                if start < width:
                    weight[pl.ds(start, width - start), :] = jnp.zeros((width - start, part), BF16)

            taken += len(piece)

        out[:tokens, :] += nt(mine[...], weight[...])
        out[tokens:, :] += nt(partner[...], weight[...])

    return pl.pallas_call(
        body,
        grid_spec=pltpu.PrefetchScalarGridSpec(
            num_scalar_prefetch=1,
            grid=(steps,),
            in_specs=[pl.BlockSpec((tokens, part), lambda j, info: (0, 2 * info[first + j] + info[0]))]
            * 2
            + specs
            + [whole] * len(old),
            out_specs=whole,
            scratch_shapes=[pltpu.VMEM((width, part), BF16)],
        ),
        out_shape=jax.ShapeDtypeStruct((2 * tokens, width), F32),
        compiler_params=params(VMEM_MIB),
        cost_estimate=cost(
            4 * steps * tokens * width * part, steps * part * (4 * tokens + 2 * width) + 8 * tokens * width
        ),
        name=name,
    )(info, cotangent, partner, *arrays, *old)


def finish(info, mine, other, factor, part):
    rank, wide = mine.shape
    span = wide - part

    def body(info, factor, mine, other, grad_b, grad_a):
        scale = factor[0]

        def put(first, second):
            grad_b[:, :part] = first[:, :part] * scale
            grad_b[:, part:] = second[:, :part] * scale
            grad_a[:, :span] = first[:, part:] * scale
            grad_a[:, span:] = second[:, part:] * scale

        @pl.when(info[0] == 0)
        def _():
            put(mine, other)

        @pl.when(info[0] != 0)
        def _():
            put(other, mine)

    whole = pl.BlockSpec((rank, wide), lambda i, info: (0, 0))
    return pl.pallas_call(
        body,
        grid_spec=pltpu.PrefetchScalarGridSpec(
            num_scalar_prefetch=1,
            grid=(1,),
            in_specs=[pl.BlockSpec(memory_space=pltpu.SMEM), whole, whole],
            out_specs=[
                pl.BlockSpec((rank, 2 * part), lambda i, info: (0, 0)),
                pl.BlockSpec((rank, 2 * span), lambda i, info: (0, 0)),
            ],
        ),
        out_shape=[
            jax.ShapeDtypeStruct((rank, 2 * part), F32),
            jax.ShapeDtypeStruct((rank, 2 * span), F32),
        ],
        compiler_params=params(8),
        cost_estimate=cost(0, 16 * rank * wide),
        name="finish",
    )(info, factor, mine, other)


def make(mesh):
    n = mesh.shape["fsdp"]
    dp = mesh.shape["dp"]
    half = n // 2
    order = list(range(0, n, 2)) + list(range(n - 1, 0, -2))
    bits = n.bit_length() - 1

    def forward(a):
        return lax.ppermute(a, "fsdp", [(order[i], order[(i + 1) % n]) for i in range(n)])

    def backward(a):
        return lax.ppermute(a, "fsdp", [(order[(i + 1) % n], order[i]) for i in range(n)])

    def over(a, axis, bit):
        return lax.ppermute(a, axis, [(i, i ^ bit) for i in range(mesh.shape[axis])])

    def shards(latent, cotangent, quant, scales, adapter_down, adapter_up):
        tokens = cotangent.shape[0]
        width, own = quant.shape
        rank = adapter_up.shape[0]
        part = own // 2
        given = width * 3 // 8
        ring = width - given
        device = lax.axis_index("dp")
        core = device & 1
        x = (device >> 1) & 1
        me = lax.axis_index("fsdp")
        place = jnp.where(me & 1 == 0, me >> 1, n - 1 - (me >> 1))

        def shard(offset):
            spot = (place + offset + n) & (n - 1)
            return jnp.where(spot < half, 2 * spot, 2 * (n - 1 - spot) + 1)

        offsets = [s * h for h in range(1, half) for s in (-1, 1)]
        offsets = [0] + offsets[:-2] + [-half] + offsets[-2:]
        shard_of = shard(np.array(offsets, np.int32))
        flipped = sum(((shard_of >> k) & 1) << (bits - 1 - k) for k in range(bits))
        info = jnp.concatenate([jnp.stack([core, x]), shard_of, flipped]).astype(jnp.int32)

        my_quant = lax.dynamic_slice_in_dim(quant, core * part, part, 1)
        my_scales = jnp.where(core == 0, scales[:, : part // BLOCK], scales[:, part // BLOCK :])
        my_up = lax.dynamic_slice_in_dim(adapter_up, core * part, part, 1)
        weight = (
            my_quant.astype(F32) * jnp.repeat(jnp.repeat(my_scales, BLOCK, axis=0), BLOCK, axis=1)
        ).astype(BF16)
        shared = weight[given:ring]
        ends = (weight[:given], weight[ring:])
        chunk = jnp.concatenate([my_up, jnp.where(x == 0, ends[0], ends[1]), shared], axis=0)
        missing = jnp.where(x == 0, ends[1], ends[0])

        stay = rank + given
        cut = max(given, ring // 2)

        def give(front, rear):
            return over(jnp.concatenate([front[rank:stay], rear[rank:stay]], axis=0), "dp", 2)

        partner = over(cotangent, "dp", 1)
        latent_partner = over(latent, "dp", 1)
        chunks, gifts = {0: chunk}, {}

        span = width // 2
        halves = jnp.concatenate(
            [lax.dynamic_slice_in_dim(a, core * span, span, 1) for a in (latent, latent_partner)], axis=0
        )

        low, low_partner = [
            lax.dot_general(adapter_down, a, (((0,), (1,)), ((), ())), preferred_element_type=F32).astype(BF16)
            for a in (latent, latent_partner)
        ]
        total_b, send = terms_b(info, cotangent, partner, low, low_partner, n)
        arrived = over(send, "dp", 2)

        chunks[-1], chunks[1] = together(forward(chunk), backward(chunk), send)[:2]
        far_up = lax.ppermute(
            together(my_up, chunks[1])[0], "fsdp", [(order[i], order[(i + half) % n]) for i in range(n)]
        )
        chunks[-2], chunks[2] = forward(chunks[-1]), backward(chunks[1])

        def ups_of(hop):
            return [[(chunks[s * hop], rank, 0, range(rank))] for s in (-1, 1)]

        def product(first, pieces, begun, name):
            return products(info, 2 + first, cotangent, partner, pieces, begun, n, name)

        sums = product(0, [[(chunk, rank, 0, range(rank))]] + ups_of(1), None, "through_first")
        front, rear, arrived, sums = together(chunks[-1], chunks[1], arrived, sums)
        gifts[1] = give(front, rear)

        def rows_of(hop):
            return [
                [
                    (chunks[s * hop], rank + ring, 0, range(rank, rank + ring)),
                    (gifts[hop], given, (s + 1) // 2, range(given)),
                ]
                for s in (-1, 1)
            ]

        own = [
            (chunk, rank + ring, 0, range(rank, rank + ring)),
            (missing, given, 0, range(given)),
        ]
        def halve(total, bit):
            size = total.shape[1] // 2
            side = (me // bit) & 1
            return (
                lax.dynamic_slice_in_dim(total, (1 - side) * size, size, 1).astype(BF16),
                lax.dynamic_slice_in_dim(total, side * size, size, 1),
            )

        sent, total_b = halve(total_b + arrived.astype(F32), 1)

        done = product(0, [own] + rows_of(1), None, "first")
        for hop in range(3, half):
            chunks[-hop], chunks[hop] = forward(chunks[1 - hop]), backward(chunks[hop - 1])
            gifts[hop - 1] = give(chunks[1 - hop], chunks[hop - 1])
            if hop < half - 1:
                chunks[-hop], chunks[hop], gifts[hop - 1], done = together(
                    chunks[-hop], chunks[hop], gifts[hop - 1], done
                )
                done = product(2 * hop - 3, rows_of(hop - 1), done, "middle")

        pieces = []
        for k in range(2, half - 1):
            pieces += ups_of(k)
        pieces += [[(far_up, rank, 0, range(rank))]]
        sums = product(3, pieces, sums, "through_second")
        part_b = over(together(sent, chunks[-2])[0], "fsdp", 1)
        hop = half - 1
        chunks[-hop], chunks[hop], done, sums = together(chunks[-hop], chunks[hop], done, sums)
        gift, front, rear = assemble(
            [(chunks[k * hop], rank, given) for k in (-1, 1)],
            [(chunks[-hop], rank, cut)],
            [(chunks[hop], rank + cut, ring - cut)],
        )
        gifts[hop] = over(gift, "dp", 2)
        sums, gift = together(sums, gift)
        both_sums = product(2 * hop, ups_of(hop), sums, "through_last")
        others = over(both_sums, "dp", 1)
        part_b = together(part_b, both_sums)[0]
        swapped = jnp.concatenate([others[tokens:], others[:tokens]], axis=0)
        through = (both_sums + swapped).astype(BF16)

        total_a = tn(through, halves)
        through = through[:tokens]
        part_a = over(total_a, "fsdp", 1)
        done = product(2 * hop - 3, rows_of(hop - 1), done, "middle")

        total_a, total_b = total_a + part_a, total_b + part_b.astype(F32)
        sent, total_b = halve(total_b, 2)
        front, rear, total_a, sent, done = together(
            forward(front), backward(rear), total_a, sent, done
        )
        gifts[half] = over(front[:given], "dp", 2)
        part_a, part_b = over(total_a, "fsdp", 2), over(sent, "fsdp", 2)
        part_a, part_b, done, gifts[hop] = together(part_a, part_b, done, gifts[hop])
        total_a, total_b = total_a + part_a, total_b + part_b.astype(F32)
        done = product(2 * half - 2, rows_of(half - 1), done, "late")
        bit = 4
        while bit < n:
            total_a = total_a + over(total_a, "fsdp", bit)
            sent, total_b = halve(total_b, bit)
            total_b = total_b + over(sent, "fsdp", bit).astype(F32)
            bit *= 2
        bit = 4
        while bit < dp:
            total_a = total_a + over(total_a, "dp", bit)
            total_b = total_b + over(total_b, "dp", bit)
            bit *= 2
        total_a, total_b, gifts[half], done = together(total_a, total_b, gifts[half], done)
        totals = jnp.concatenate([total_b, total_a], axis=1)
        others = over(totals, "dp", 2)
        last = [
            (front, cut, 0, range(cut)),
            (rear, ring - cut, 0, range(ring - cut)),
            (gifts[half], given, 0, range(given)),
        ]
        done = product(2 * half - 3, [last], done, "last")
        others, done = together(others, done)
        other_b, total_a = others[:, : part // 2], total_a + others[:, part // 2 :]
        low_x, high_x = jnp.where(x == 0, total_b, other_b), jnp.where(x == 0, other_b, total_b)
        ends = jnp.concatenate([low_x, high_x, total_a], axis=1)
        other_ends = over(ends, "dp", 1)
        factor = 1.0 / jnp.sqrt(F32(tokens * dp * n))
        grad_b, grad_a = finish(info, ends, other_ends, factor.reshape(1), part)
        grad_a = grad_a.T

        frozen = done[:tokens] + over(done[tokens:], "dp", 1)
        begin, middle, end = frozen[:, :given], frozen[:, given:ring], frozen[:, ring:]
        frozen = jnp.concatenate(
            [jnp.where(x == 0, begin, end), middle, jnp.where(x == 0, end, begin)], axis=1
        )
        latent_gradient = (frozen + nt(through, adapter_down)).astype(BF16)
        return (latent_gradient, grad_a, grad_b)

    return shards


def solution(mesh):
    placed = (
        P(("dp", "fsdp"), None),
        P(("dp", "fsdp"), None),
        P(None, "fsdp"),
        P(None, "fsdp"),
        P(),
        P(None, "fsdp"),
    )
    return jax.shard_map(
        make(mesh),
        mesh=mesh,
        in_specs=placed,
        out_specs=(P(("dp", "fsdp"), None), P(), P(None, "fsdp")),
        check_vma=False,
    )
```

```python
import jax
import jax.numpy as jnp
import numpy as np
from jax import lax
from jax.experimental import pallas as pl
from jax.experimental.pallas import tpu as pltpu
from jax.sharding import PartitionSpec as P

BLOCK = 128
F32 = jnp.float32
BF16 = jnp.bfloat16
MIB = 1 << 20
VMEM_MIB = 50


def nt(left, right):
    return lax.dot_general(left, right, (((1,), (1,)), ((), ())), preferred_element_type=F32)


def nn(left, right):
    return jnp.dot(left, right, preferred_element_type=F32)


def tn(left, right):
    return lax.dot_general(left, right, (((0,), (0,)), ((), ())), preferred_element_type=F32)


def params(mib):
    return pltpu.CompilerParams(vmem_limit_bytes=mib * MIB)


def cost(flops, nbytes):
    return pl.CostEstimate(flops=flops, bytes_accessed=nbytes, transcendentals=0)


def together(*arrays):
    return lax.optimization_barrier(arrays)


def assemble(*outputs):
    pieces = [piece for output in outputs for piece in output]
    where = [
        (at, sum(count for _, _, count in output[:k]))
        for at, output in enumerate(outputs)
        for k in range(len(output))
    ]

    def body(*refs):
        ins, outs, semaphore = refs[: len(pieces)], refs[len(pieces) : -1], refs[-1]
        copies = [
            pltpu.make_async_copy(
                ins[k].at[pl.ds(start, count)], outs[to].at[pl.ds(row, count)], semaphore.at[k]
            )
            for k, ((_, start, count), (to, row)) in enumerate(zip(pieces, where))
        ]
        for copy in copies:
            copy.start()
        for copy in copies:
            copy.wait()

    return pl.pallas_call(
        body,
        in_specs=[pl.BlockSpec(memory_space=pl.ANY)] * len(pieces),
        out_specs=[pl.BlockSpec(memory_space=pl.ANY)] * len(outputs),
        out_shape=[
            jax.ShapeDtypeStruct((sum(c for _, _, c in output), output[0][0].shape[1]), BF16)
            for output in outputs
        ],
        scratch_shapes=[pltpu.SemaphoreType.DMA((len(pieces),))],
        compiler_params=params(1),
        cost_estimate=cost(0, 4 * sum(c * a.shape[1] for a, _, c in pieces)),
        name="assemble",
    )(*[a for a, _, _ in pieces])


def terms_b(info, cotangent, partner, low, low_partner, n):
    tokens, columns = cotangent.shape
    part = columns // n // 2
    span = part // 2
    rank = low.shape[0]

    def body(info, mine, partner, low, low_partner, keep, send):
        x = info[1]

        def term(which):
            here = pl.ds(pl.multiple_of(which * span, BLOCK), span)
            return nn(low[...], mine[:, here]) + nn(low_partner[...], partner[:, here])

        keep[...] = term(x)
        send[...] = term(1 - x).astype(send.dtype)

    return pl.pallas_call(
        body,
        grid_spec=pltpu.PrefetchScalarGridSpec(
            num_scalar_prefetch=1,
            grid=(n,),
            in_specs=[pl.BlockSpec((tokens, part), lambda j, info: (0, 2 * info[2 + j] + info[0]))] * 2
            + [pl.BlockSpec((rank, tokens), lambda j, info: (0, 0))] * 2,
            out_specs=[pl.BlockSpec((rank, span), lambda j, info: (0, info[2 + n + j]))] * 2,
        ),
        out_shape=[
            jax.ShapeDtypeStruct((rank, n * span), F32),
            jax.ShapeDtypeStruct((rank, n * span), BF16),
        ],
        compiler_params=params(VMEM_MIB),
        cost_estimate=cost(4 * tokens * rank * n * part, tokens * n * part * 4),
        name="terms_b",
    )(info, cotangent, partner, low, low_partner)


def products(info, first, cotangent, partner, pieces, begun, n, name):
    tokens, columns = cotangent.shape
    part = columns // n // 2
    steps = len(pieces)
    arrays = [rows[0] for piece in pieces for rows in piece]
    specs = [
        pl.BlockSpec((block, part), lambda j, info, which=which: (which, 0))
        for piece in pieces
        for _, block, which, _ in piece
    ]
    width = sum(rows.stop - rows.start for _, _, _, rows in pieces[0])
    old = [] if begun is None else [begun]
    whole = pl.BlockSpec((2 * tokens, width), lambda j, info: (0, 0))

    def body(info, mine, partner, *refs):
        row_refs, old_refs, (out, weight) = refs[: len(arrays)], refs[len(arrays) : -2], refs[-2:]
        at = pl.program_id(0)

        @pl.when(at == 0)
        def _():
            out[...] = old_refs[0][...] if old_refs else jnp.zeros_like(out)

        taken = 0
        for j, piece in enumerate(pieces):

            @pl.when(at == j)
            def _(piece=piece, taken=taken):
                start = 0
                for k, (_, _, _, rows) in enumerate(piece):
                    count = rows.stop - rows.start
                    weight[pl.ds(start, count), :] = row_refs[taken + k][pl.ds(rows.start, count), :]
                    start += count
                if start < width:
                    weight[pl.ds(start, width - start), :] = jnp.zeros((width - start, part), BF16)

            taken += len(piece)

        out[:tokens, :] += nt(mine[...], weight[...])
        out[tokens:, :] += nt(partner[...], weight[...])

    return pl.pallas_call(
        body,
        grid_spec=pltpu.PrefetchScalarGridSpec(
            num_scalar_prefetch=1,
            grid=(steps,),
            in_specs=[pl.BlockSpec((tokens, part), lambda j, info: (0, 2 * info[first + j] + info[0]))]
            * 2
            + specs
            + [whole] * len(old),
            out_specs=whole,
            scratch_shapes=[pltpu.VMEM((width, part), BF16)],
        ),
        out_shape=jax.ShapeDtypeStruct((2 * tokens, width), F32),
        compiler_params=params(VMEM_MIB),
        cost_estimate=cost(
            4 * steps * tokens * width * part, steps * part * (4 * tokens + 2 * width) + 8 * tokens * width
        ),
        name=name,
    )(info, cotangent, partner, *arrays, *old)


def finish(info, mine, other, factor, part):
    rank, wide = mine.shape
    span = wide - part

    def body(info, factor, mine, other, grad_b, grad_a):
        scale = factor[0]

        def put(first, second):
            grad_b[:, :part] = first[:, :part] * scale
            grad_b[:, part:] = second[:, :part] * scale
            grad_a[:, :span] = first[:, part:] * scale
            grad_a[:, span:] = second[:, part:] * scale

        @pl.when(info[0] == 0)
        def _():
            put(mine, other)

        @pl.when(info[0] != 0)
        def _():
            put(other, mine)

    whole = pl.BlockSpec((rank, wide), lambda i, info: (0, 0))
    return pl.pallas_call(
        body,
        grid_spec=pltpu.PrefetchScalarGridSpec(
            num_scalar_prefetch=1,
            grid=(1,),
            in_specs=[pl.BlockSpec(memory_space=pltpu.SMEM), whole, whole],
            out_specs=[
                pl.BlockSpec((rank, 2 * part), lambda i, info: (0, 0)),
                pl.BlockSpec((rank, 2 * span), lambda i, info: (0, 0)),
            ],
        ),
        out_shape=[
            jax.ShapeDtypeStruct((rank, 2 * part), F32),
            jax.ShapeDtypeStruct((rank, 2 * span), F32),
        ],
        compiler_params=params(8),
        cost_estimate=cost(0, 16 * rank * wide),
        name="finish",
    )(info, factor, mine, other)


def make(mesh):
    n = mesh.shape["fsdp"]
    dp = mesh.shape["dp"]
    half = n // 2
    order = list(range(0, n, 2)) + list(range(n - 1, 0, -2))
    bits = n.bit_length() - 1

    def forward(a):
        return lax.ppermute(a, "fsdp", [(order[i], order[(i + 1) % n]) for i in range(n)])

    def backward(a):
        return lax.ppermute(a, "fsdp", [(order[(i + 1) % n], order[i]) for i in range(n)])

    def over(a, axis, bit):
        return lax.ppermute(a, axis, [(i, i ^ bit) for i in range(mesh.shape[axis])])

    def shards(latent, cotangent, quant, scales, adapter_down, adapter_up):
        tokens = cotangent.shape[0]
        width, own = quant.shape
        rank = adapter_up.shape[0]
        part = own // 2
        given = width * 3 // 8
        ring = width - given
        device = lax.axis_index("dp")
        core = device & 1
        x = (device >> 1) & 1
        me = lax.axis_index("fsdp")
        place = jnp.where(me & 1 == 0, me >> 1, n - 1 - (me >> 1))

        def shard(offset):
            spot = (place + offset + n) & (n - 1)
            return jnp.where(spot < half, 2 * spot, 2 * (n - 1 - spot) + 1)

        offsets = [s * h for h in range(1, half) for s in (-1, 1)]
        offsets = [0] + offsets[:-2] + [-half] + offsets[-2:]
        shard_of = shard(np.array(offsets, np.int32))
        flipped = sum(((shard_of >> k) & 1) << (bits - 1 - k) for k in range(bits))
        info = jnp.concatenate([jnp.stack([core, x]), shard_of, flipped]).astype(jnp.int32)

        my_quant = lax.dynamic_slice_in_dim(quant, core * part, part, 1)
        my_scales = jnp.where(core == 0, scales[:, : part // BLOCK], scales[:, part // BLOCK :])
        my_up = lax.dynamic_slice_in_dim(adapter_up, core * part, part, 1)
        weight = (
            my_quant.astype(F32) * jnp.repeat(jnp.repeat(my_scales, BLOCK, axis=0), BLOCK, axis=1)
        ).astype(BF16)
        shared = weight[given:ring]
        ends = (weight[:given], weight[ring:])
        chunk = jnp.concatenate([my_up, jnp.where(x == 0, ends[0], ends[1]), shared], axis=0)
        missing = jnp.where(x == 0, ends[1], ends[0])

        stay = rank + given
        cut = max(given, ring // 2)

        def give(front, rear):
            return over(jnp.concatenate([front[rank:stay], rear[rank:stay]], axis=0), "dp", 2)

        partner = over(cotangent, "dp", 1)
        latent_partner = over(latent, "dp", 1)
        chunks, gifts = {0: chunk}, {}

        span = width // 2
        halves = jnp.concatenate(
            [lax.dynamic_slice_in_dim(a, core * span, span, 1) for a in (latent, latent_partner)], axis=0
        )

        low, low_partner = [
            lax.dot_general(adapter_down, a, (((0,), (1,)), ((), ())), preferred_element_type=F32).astype(BF16)
            for a in (latent, latent_partner)
        ]
        total_b, send = terms_b(info, cotangent, partner, low, low_partner, n)
        arrived = over(send, "dp", 2)

        chunks[-1], chunks[1] = together(forward(chunk), backward(chunk), send)[:2]
        far_up = lax.ppermute(
            together(my_up, chunks[1])[0], "fsdp", [(order[i], order[(i + half) % n]) for i in range(n)]
        )
        chunks[-2], chunks[2] = forward(chunks[-1]), backward(chunks[1])

        def ups_of(hop):
            return [[(chunks[s * hop], rank, 0, range(rank))] for s in (-1, 1)]

        def product(first, pieces, begun, name):
            return products(info, 2 + first, cotangent, partner, pieces, begun, n, name)

        sums = product(0, [[(chunk, rank, 0, range(rank))]] + ups_of(1), None, "through_first")
        front, rear, arrived, sums = together(chunks[-1], chunks[1], arrived, sums)
        gifts[1] = give(front, rear)

        def rows_of(hop):
            return [
                [
                    (chunks[s * hop], rank + ring, 0, range(rank, rank + ring)),
                    (gifts[hop], given, (s + 1) // 2, range(given)),
                ]
                for s in (-1, 1)
            ]

        own = [
            (chunk, rank + ring, 0, range(rank, rank + ring)),
            (missing, given, 0, range(given)),
        ]
        def halve(total, bit):
            size = total.shape[1] // 2
            side = (me // bit) & 1
            return (
                lax.dynamic_slice_in_dim(total, (1 - side) * size, size, 1).astype(BF16),
                lax.dynamic_slice_in_dim(total, side * size, size, 1),
            )

        sent, total_b = halve(total_b + arrived.astype(F32), 1)

        done = product(0, [own] + rows_of(1), None, "first")
        for hop in range(3, half):
            chunks[-hop], chunks[hop] = forward(chunks[1 - hop]), backward(chunks[hop - 1])
            gifts[hop - 1] = give(chunks[1 - hop], chunks[hop - 1])
            if hop < half - 1:
                chunks[-hop], chunks[hop], gifts[hop - 1], done = together(
                    chunks[-hop], chunks[hop], gifts[hop - 1], done
                )
                done = product(2 * hop - 3, rows_of(hop - 1), done, "middle")

        pieces = []
        for k in range(2, half - 1):
            pieces += ups_of(k)
        pieces += [[(far_up, rank, 0, range(rank))]]
        sums = product(3, pieces, sums, "through_second")
        part_b = over(together(sent, chunks[-2])[0], "fsdp", 1)
        hop = half - 1
        chunks[-hop], chunks[hop], done, sums = together(chunks[-hop], chunks[hop], done, sums)
        gift, front, rear = assemble(
            [(chunks[k * hop], rank, given) for k in (-1, 1)],
            [(chunks[-hop], rank, cut)],
            [(chunks[hop], rank + cut, ring - cut)],
        )
        gifts[hop] = over(gift, "dp", 2)
        sums, gift = together(sums, gift)
        both_sums = product(2 * hop, ups_of(hop), sums, "through_last")
        others = over(both_sums, "dp", 1)
        part_b = together(part_b, both_sums)[0]
        swapped = jnp.concatenate([others[tokens:], others[:tokens]], axis=0)
        through = (both_sums + swapped).astype(BF16)

        total_a = tn(through, halves)
        through = through[:tokens]
        part_a = over(total_a, "fsdp", 1)
        done = product(2 * hop - 3, rows_of(hop - 1), done, "middle")

        total_a, total_b = total_a + part_a, total_b + part_b.astype(F32)
        sent, total_b = halve(total_b, 2)
        front, rear, total_a, sent, done = together(
            forward(front), backward(rear), total_a, sent, done
        )
        gifts[half] = over(front[:given], "dp", 2)
        part_a, part_b = over(total_a, "fsdp", 2), over(sent, "fsdp", 2)
        part_a, part_b, done, gifts[hop] = together(part_a, part_b, done, gifts[hop])
        total_a, total_b = total_a + part_a, total_b + part_b.astype(F32)
        bit = 4
        while bit < n:
            total_a = total_a + over(total_a, "fsdp", bit)
            sent, total_b = halve(total_b, bit)
            total_b = total_b + over(sent, "fsdp", bit).astype(F32)
            bit *= 2
        bit = 4
        while bit < dp:
            total_a = total_a + over(total_a, "dp", bit)
            total_b = total_b + over(total_b, "dp", bit)
            bit *= 2
        total_a, total_b, gifts[half], done = together(total_a, total_b, gifts[half], done)
        done = product(2 * half - 2, rows_of(half - 1), done, "late")
        totals = jnp.concatenate([total_b, total_a], axis=1)
        others = over(totals, "dp", 2)
        last = [
            (front, cut, 0, range(cut)),
            (rear, ring - cut, 0, range(ring - cut)),
            (gifts[half], given, 0, range(given)),
        ]
        done = product(2 * half - 3, [last], done, "last")
        others, done = together(others, done)
        other_b, total_a = others[:, : part // 2], total_a + others[:, part // 2 :]
        low_x, high_x = jnp.where(x == 0, total_b, other_b), jnp.where(x == 0, other_b, total_b)
        ends = jnp.concatenate([low_x, high_x, total_a], axis=1)
        other_ends = over(ends, "dp", 1)
        factor = 1.0 / jnp.sqrt(F32(tokens * dp * n))
        grad_b, grad_a = finish(info, ends, other_ends, factor.reshape(1), part)
        grad_a = grad_a.T

        frozen = done[:tokens] + over(done[tokens:], "dp", 1)
        begin, middle, end = frozen[:, :given], frozen[:, given:ring], frozen[:, ring:]
        frozen = jnp.concatenate(
            [jnp.where(x == 0, begin, end), middle, jnp.where(x == 0, end, begin)], axis=1
        )
        latent_gradient = (frozen + nt(through, adapter_down)).astype(BF16)
        return (latent_gradient, grad_a, grad_b)

    return shards


def solution(mesh):
    placed = (
        P(("dp", "fsdp"), None),
        P(("dp", "fsdp"), None),
        P(None, "fsdp"),
        P(None, "fsdp"),
        P(),
        P(None, "fsdp"),
    )
    return jax.shard_map(
        make(mesh),
        mesh=mesh,
        in_specs=placed,
        out_specs=(P(("dp", "fsdp"), None), P(), P(None, "fsdp")),
        check_vma=False,
    )
```
